32 devices in a mesh: groups: 2 (over x), seq: 16 (over z, y, core).
Axes of the slice: x: 2, y: 2, z: 4, core: 2. Of those that a mesh axis runs over, the one named last changes fastest.
Arguments:
- latent_noise: float32 [4096, 192], P(('groups', 'seq')), parts along dimension 0, may hold values from -6 to 6
- position: bfloat16 [2048, 768], P('seq'), may hold values from -2 to 2
- in_weight: bfloat16 [192, 768], replicated, may hold values from -0.4375 to 0.4375
- gain_attn: float32 [768], replicated, may hold values from 0.1 to 1.9
- query_weight: bfloat16 [768, 384], replicated, may hold values from -5.1 to 5.1
- key_weight: bfloat16 [768, 384], replicated, may hold values from -5.1 to 5.1
- value_weight: bfloat16 [768, 384], replicated, may hold values from -0.21875 to 0.21875
- mix_weight: bfloat16 [384, 768], replicated, may hold values from -0.3125 to 0.3125
- gain_mlp: float32 [768], replicated, may hold values from 0.1 to 1.9
- up_weight: bfloat16 [768, 1536], replicated, may hold values from -0.21875 to 0.21875
- down_weight: bfloat16 [1536, 768], replicated, may hold values from -0.15625 to 0.15625
- gain_out: float32 [768], replicated, may hold values from 0.1 to 1.9
- out_weight: bfloat16 [768, 384], replicated, may hold values from -0.15625 to 0.15625
Outputs:
- sample: float32 [4096, 192], P(('groups', 'seq')), parts along dimension 0
The draws below stay inside these ranges and needn't reach their ends.
There are 2 independent parts, one for each index of `groups`. The reference program is written for one: setup_inputs(seed, part) draws one part's arguments, and reference() takes and returns one part's arrays. A program takes and returns all parts, laid end to end along the dimension named above; an argument that names none is the same for every part. Nothing has to cross between parts.
All inputs are finite; a program needn't handle non-finite values.
Results may differ from the reference program's by a relative error of at most 0.04.
Values may be sent and summed in bfloat16 or wider, within the bound.
A program may use at most 128 MiB of HBM per device.

```python
import math
import jax
import jax.numpy as jnp
from jax import lax

PATCH = 192
D = 768
HEADS = 6
HD = 64
FF = 1536
ITERS = 2
SEQ = 2048


def paired_projections(key):
    base_key = jax.random.fold_in(key, 7301)
    other_key = jax.random.fold_in(key, 7302)
    base = jnp.clip(jax.random.normal(base_key, (D, HEADS * HD), jnp.float32), -4.0, 4.0)
    other = jnp.clip(jax.random.normal(other_key, (D, HEADS * HD), jnp.float32), -4.0, 4.0)
    factor = 2.0 / math.sqrt(D)
    return (base * factor, other * factor)


def draw_query_weight(key, part):
    return paired_projections(key)[0].astype(jnp.bfloat16)


def draw_key_weight(key, part):
    return paired_projections(key)[1].astype(jnp.bfloat16)


def block_scale(rng, dims, cuts, low, largest):
    level, own = 1.0, jax.random.fold_in(rng, 6)
    for dim, parts in cuts:
        steps = jnp.exp(jax.random.uniform(jax.random.fold_in(own, dim), (parts,), jnp.float32, low / len(cuts), largest / len(cuts)))
        level = level * jnp.repeat(steps, dims[dim] // parts).reshape([-1 if axis == dim else 1 for axis in range(len(dims))])
    return level


def normal_values(key, dims, width, reach, shards=(), kind=jnp.bfloat16):
    result = width * jax.random.normal(key, dims, jnp.float32)
    if shards:
        result = result * block_scale(key, dims, shards, -0.22, 0.18)
    return jnp.clip(result, -reach, reach).astype(kind)


def setup_inputs(seed: int = 0, part: int = 0) -> dict:
    keys = jax.random.split(jax.random.key(seed), 14)
    part_keys = jax.random.split(jax.random.fold_in(keys[13], part), 14)
    return {
        "latent_noise": normal_values(part_keys[0], (SEQ, PATCH), 1.0, 6.0, ((0, 16),), jnp.float32),
        "position": normal_values(keys[1], (SEQ, D), 0.25, 2.0, ((0, 16),)),
        "in_weight": normal_values(keys[2], (PATCH, D), PATCH ** -0.5, 0.4375),
        "gain_attn": jnp.clip(1.0 + 0.18 * jax.random.normal(keys[3], (D,), jnp.float32), 0.1, 1.9),
        "query_weight": draw_query_weight(jax.random.fold_in(keys[13], 71), part),
        "key_weight": draw_key_weight(jax.random.fold_in(keys[13], 71), part),
        "value_weight": normal_values(keys[6], (D, HEADS * HD), D ** -0.5, 0.21875),
        "mix_weight": normal_values(keys[7], (HEADS * HD, D), (HEADS * HD) ** -0.5, 0.3125),
        "gain_mlp": jnp.clip(1.0 + 0.18 * jax.random.normal(keys[8], (D,), jnp.float32), 0.1, 1.9),
        "up_weight": normal_values(keys[9], (D, FF), D ** -0.5, 0.21875),
        "down_weight": normal_values(keys[10], (FF, D), FF ** -0.5, 0.15625),
        "gain_out": jnp.clip(1.0 + 0.18 * jax.random.normal(keys[11], (D,), jnp.float32), 0.1, 1.9),
        "out_weight": normal_values(keys[12], (D, 2 * PATCH), (2 * D) ** -0.5, 0.15625),
    }


def rms_norm(values, gain):
    scale = lax.rsqrt(lax.optimization_barrier(jnp.mean(values * values, axis=-1, keepdims=True)) + 1e-06)
    return values * scale * gain

def attend(query_rows, key_rows, value_rows):
    block_rows = math.gcd(SEQ, 512)
    pieces = []
    for first_row in range(0, SEQ, block_rows):
        end_row = first_row + block_rows
        query_heads = query_rows[first_row:end_row].astype(jnp.float32).reshape(block_rows, HEADS, HD)
        key_heads = key_rows[:end_row].astype(jnp.float32).reshape(end_row, HEADS, HD)
        value_heads = value_rows[:end_row].astype(jnp.float32).reshape(end_row, HEADS, HD)
        scores = jnp.einsum('qhd,khd->hqk', query_heads, key_heads, precision=lax.Precision.HIGHEST) * HD ** (-0.5)
        query_pos = first_row + jnp.arange(block_rows, dtype=jnp.int32)
        key_pos = jnp.arange(end_row, dtype=jnp.int32)
        causal = (key_pos[None, :] <= query_pos[:, None])[None]
        masked = jnp.where(causal, scores, -1e+30)
        row_max = lax.optimization_barrier(jnp.max(masked, axis=2, keepdims=True))
        weights = jnp.where(causal, jnp.exp(masked - row_max), 0.0)
        totals = lax.optimization_barrier(jnp.sum(weights, axis=2, keepdims=True))
        rounded = weights.astype(jnp.bfloat16).astype(jnp.float32)
        attended = jnp.einsum('hqk,khd->hqd', rounded, value_heads, precision=lax.Precision.HIGHEST) / totals
        pieces.append(jnp.transpose(attended, (1, 0, 2)).reshape(block_rows, HEADS * HD))
    return jnp.concatenate(pieces, axis=0).astype(jnp.bfloat16)

def jacobi_step(current, latent_noise, position, in_weight, gain_attn, query_weight, key_weight, value_weight, mix_weight, gain_mlp, up_weight, down_weight, gain_out, out_weight):
    shifted = jnp.concatenate([jnp.zeros((1, PATCH), current.dtype), current[:-1]], axis=0)
    hidden_in = jnp.dot(shifted.astype(jnp.bfloat16), in_weight, preferred_element_type=jnp.float32) + position.astype(jnp.float32)
    normed_attn = rms_norm(hidden_in, gain_attn).astype(jnp.bfloat16)
    query_rows = jnp.dot(normed_attn, query_weight, preferred_element_type=jnp.float32).astype(jnp.bfloat16)
    key_rows = jnp.dot(normed_attn, key_weight, preferred_element_type=jnp.float32).astype(jnp.bfloat16)
    value_rows = jnp.dot(normed_attn, value_weight, preferred_element_type=jnp.float32).astype(jnp.bfloat16)
    attended = attend(query_rows, key_rows, value_rows)
    hidden_mid = hidden_in + jnp.dot(attended, mix_weight, preferred_element_type=jnp.float32)
    normed_mlp = rms_norm(hidden_mid, gain_mlp).astype(jnp.bfloat16)
    activated = jax.nn.gelu(jnp.dot(normed_mlp, up_weight, preferred_element_type=jnp.float32)).astype(jnp.bfloat16)
    hidden_out = hidden_mid + jnp.dot(activated, down_weight, preferred_element_type=jnp.float32)
    normed_out = rms_norm(hidden_out, gain_out).astype(jnp.bfloat16)
    statistics = jnp.dot(normed_out, out_weight, preferred_element_type=jnp.float32)
    mean_shift = statistics[:, :PATCH]
    log_scale = statistics[:, PATCH:]
    return latent_noise * jnp.exp(log_scale) + mean_shift

def reference(latent_noise, position, in_weight, gain_attn, query_weight, key_weight, value_weight, mix_weight, gain_mlp, up_weight, down_weight, gain_out, out_weight):
    current = latent_noise
    for iteration in range(ITERS):
        current = jacobi_step(current, latent_noise, position, in_weight, gain_attn, query_weight, key_weight, value_weight, mix_weight, gain_mlp, up_weight, down_weight, gain_out, out_weight)
    return current[::-1]
```

```python
import functools

import jax
import jax.numpy as jnp
from jax import lax
from jax.experimental import pallas as pl
from jax.experimental.pallas import tpu as pltpu
from jax.sharding import PartitionSpec as P

HEADS = 6
ITERS = 2
COLS = 4
DOWN, ACROSS, CORE, CORE_FAR = range(4)
TAIL = 16
F32, BF16 = jnp.float32, jnp.bfloat16


def dot(a, b):
    return jnp.dot(a, b, preferred_element_type=F32)


def dot_nt(a, b):
    return lax.dot_general(a, b, (((1,), (1,)), ((), ())), preferred_element_type=F32)


def rms_norm(values, gain):
    scale = lax.rsqrt(jnp.mean(values * values, axis=-1, keepdims=True) + 1e-06)
    return values * scale * gain


def kernel(
    n,
    latent,
    gain_attn,
    gain_mlp,
    gain_out,
    position,
    *refs,
):
    hbm = refs[:8]
    out = refs[8]
    scratch = refs[9:]
    in_w, q_w, k_w, v_w, mix_w, up_w, down_w, out_w = vmem = scratch[:8]
    (
        blocks,
        places,
        tail_src,
        tail_dst,
        queries,
        top,
        total,
        acc,
        current,
        flip_src,
        flip_dst,
        load_sem,
        send_sem,
        recv_sem,
        tail_send,
        tail_recv,
        flip_send,
        flip_recv,
    ) = scratch[8:]
    rows, patch = latent.shape
    width = q_w.shape[1]
    head_dim = width // HEADS
    pair = 2 * head_dim
    pairs = HEADS // 2
    line = n // COLS
    me = lax.axis_index("seq")
    row, col = me // COLS, me % COLS
    across = row * COLS + (col + 2) % COLS
    other = me + 1 - 2 * (me % 2)
    mirror = n - 1 - me

    loads = [
        pltpu.make_async_copy(source, target, load_sem.at[i])
        for i, (source, target) in enumerate(zip(hbm, vmem))
    ]
    own_rows = pl.ds(pl.multiple_of(me * rows, rows), rows)
    place_load = pltpu.make_async_copy(position, places.at[own_rows], load_sem.at[len(loads)])
    place_load.start()
    for load in loads:
        load.start()

    barrier = pltpu.get_barrier_semaphore()

    def greet(device):
        pl.semaphore_signal(barrier, inc=1, device_id={"seq": device}, device_id_type=pl.DeviceIdType.MESH)

    greet(across)
    greet(other)
    greet(mirror)
    pl.when(row > 0)(lambda: greet(me - COLS))
    pl.when(row < line - 1)(lambda: greet(me + COLS))
    pl.when(me > 0)(lambda: greet(me - 1))
    pl.when(me < n - 1)(lambda: greet(me + 1))

    def hop(payload, kind, which):
        column = (col + 2) % COLS if kind == CORE_FAR else col
        return remote(payload, kind, which, column)

    def landing(payload, kind, which):
        beside = col + 1 - 2 * (col % 2)
        column = {DOWN: col, ACROSS: (col + 2) % COLS, CORE: beside, CORE_FAR: (beside + 2) % COLS}[kind]
        return remote(payload, kind, which, column)

    def remote(payload, kind, which, column):
        here = pl.ds(pl.multiple_of((which * COLS + column) * rows, rows), rows)
        ref = places.at[here] if payload == ITERS else blocks.at[payload, here]
        target = {DOWN: me + COLS, ACROSS: across, CORE: other, CORE_FAR: other}[kind]
        return pltpu.make_async_remote_copy(
            src_ref=ref,
            dst_ref=ref,
            send_sem=send_sem.at[payload, kind, which],
            recv_sem=recv_sem.at[payload, kind, which],
            device_id={"seq": target},
            device_id_type=pl.DeviceIdType.MESH,
        )

    def send_on(payload, which):
        pl.when(row < line - 1)(lambda: hop(payload, DOWN, which).start())
        hop(payload, ACROSS, which).start()
        hop(payload, CORE, which).start()

    def tail_copy(step):
        return pltpu.make_async_remote_copy(
            src_ref=tail_src.at[step],
            dst_ref=tail_dst.at[step],
            send_sem=tail_send.at[step],
            recv_sem=tail_recv.at[step],
            device_id={"seq": me + 1},
            device_id_type=pl.DeviceIdType.MESH,
        )

    current[...] = latent[...]
    place_load.wait()
    pl.semaphore_wait(
        barrier,
        3
        + (row > 0).astype(jnp.int32)
        + (row < line - 1).astype(jnp.int32)
        + (me > 0).astype(jnp.int32)
        + (me < n - 1).astype(jnp.int32),
    )

    lane = lax.broadcasted_iota(jnp.int32, (1, pair), 1)
    low = lane < head_dim

    for step in range(ITERS):
        payloads = (ITERS, 0) if step == 0 else (step,)
        value = current[...]
        tail_src[step] = value[rows - TAIL :].astype(BF16)
        pl.when(me < n - 1)(lambda: tail_copy(step).start())
        if step == 0:
            send_on(ITERS, row)
        turned = pltpu.roll(value, 1, 0)
        pl.when(me > 0)(lambda: tail_copy(step).wait_recv())

        @pl.when(me == 0)
        def _():
            tail_dst[step] = jnp.zeros_like(tail_dst[step])

        before = tail_dst[step].astype(F32)[TAIL - 1 :]
        first = lax.broadcasted_iota(jnp.int32, (rows, 1), 0) == 0
        shifted = jnp.where(first, before, turned).astype(BF16)
        blocks[step, own_rows] = shifted
        send_on(step, row)

        if step == 0:
            for load in loads[:4]:
                load.wait()
        hidden_in = dot(shifted, in_w[...]) + places[own_rows].astype(F32)
        normed = rms_norm(hidden_in, gain_attn[...]).astype(BF16)
        query = dot(normed, q_w[...]).astype(BF16).astype(F32) * head_dim ** (-0.5)
        for p in range(pairs):
            both = query[:, p * pair : (p + 1) * pair]
            queries[p, :rows] = jnp.where(low, both, 0.0).astype(BF16)
            queries[p, rows:] = jnp.where(low, 0.0, both).astype(BF16)

        def exchange(which):
            for payload in payloads:
                landing(payload, ACROSS, which).wait_recv()
                hop(payload, CORE_FAR, which).start()

            @pl.when(which > 0)
            def _():
                for payload in payloads:
                    landing(payload, DOWN, which - 1).wait_recv()
                    send_on(payload, which - 1)

            for payload in payloads:
                landing(payload, CORE, which).wait_recv()
                landing(payload, CORE_FAR, which).wait_recv()

        def attend(which, own):
            span = COLS * rows
            here = pl.ds(pl.multiple_of(which * span, span), span)
            hidden = dot(blocks[step, here], in_w[...]) + places[here].astype(F32)
            normed = rms_norm(hidden, gain_attn[...]).astype(BF16)
            keys = dot(normed, k_w[...]).astype(BF16)
            values = dot(normed, v_w[...]).astype(BF16)
            if own:
                query_pos = lax.broadcasted_iota(jnp.int32, (2 * rows, span), 0) % rows + col * rows
                key_pos = lax.broadcasted_iota(jnp.int32, (2 * rows, span), 1)
                causal = key_pos <= query_pos
            for p in range(pairs):
                columns = slice(p * pair, (p + 1) * pair)
                scores = dot_nt(queries[p], keys[:, columns])
                if own:
                    scores = jnp.where(causal, scores, -1e30)
                highest = jnp.max(scores, axis=1, keepdims=True)
                if not own:
                    old = top[p]
                    highest = jnp.maximum(old, highest)
                weights = jnp.exp(scores - highest)
                sums = jnp.sum(weights, axis=1, keepdims=True)
                product = dot(weights.astype(BF16), values[:, columns])
                if own:
                    total[p] = sums
                    acc[p] = product
                else:
                    shrink = jnp.exp(old - highest)
                    total[p] = total[p] * shrink + sums
                    acc[p] = acc[p] * shrink + product
                top[p] = highest

        exchange(row)
        attend(row, True)

        @pl.loop(0, row)
        def _(i):
            which = row - 1 - i
            exchange(which)
            attend(which, False)

        parts = []
        for p in range(pairs):
            result = acc[p] / total[p]
            parts.append(jnp.where(low, result[:rows], result[rows:]).astype(BF16))
        attended = jnp.concatenate(parts, axis=1)
        if step == 0:
            for load in loads[4:]:
                load.wait()
        hidden_mid = hidden_in + dot(attended, mix_w[...])
        normed_mlp = rms_norm(hidden_mid, gain_mlp[...]).astype(BF16)
        activated = jax.nn.gelu(dot(normed_mlp, up_w[...])).astype(BF16)
        hidden_out = hidden_mid + dot(activated, down_w[...])
        normed_out = rms_norm(hidden_out, gain_out[...]).astype(BF16)
        statistics = dot(normed_out, out_w[...])
        mean_shift = statistics[:, :patch]
        log_scale = pltpu.roll(statistics, patch, 1)[:, :patch]
        current[...] = latent[...] * jnp.exp(log_scale) + mean_shift

    flip_src[...] = current[...].astype(BF16)
    flip = pltpu.make_async_remote_copy(
        src_ref=flip_src,
        dst_ref=flip_dst,
        send_sem=flip_send,
        recv_sem=flip_recv,
        device_id={"seq": mirror},
        device_id_type=pl.DeviceIdType.MESH,
    )
    flip.start()

    for step in range(ITERS):
        pl.when(me < n - 1)(lambda: tail_copy(step).wait_send())

    @pl.loop(0, row + 1)
    def _(which):
        for payload in range(ITERS + 1):
            pl.when(row < line - 1)(lambda: hop(payload, DOWN, which).wait_send())
            for kind in (ACROSS, CORE, CORE_FAR):
                hop(payload, kind, which).wait_send()

    flip.wait()
    out[...] = flip_dst[...].astype(F32)


def per_device(
    latent_noise,
    position,
    in_weight,
    gain_attn,
    query_weight,
    key_weight,
    value_weight,
    mix_weight,
    gain_mlp,
    up_weight,
    down_weight,
    gain_out,
    out_weight,
):
    n = lax.axis_size("seq")
    rows, patch = latent_noise.shape
    model = position.shape[1]
    pair = 2 * query_weight.shape[1] // HEADS
    pairs = HEADS // 2
    weights = (
        in_weight,
        query_weight,
        key_weight,
        value_weight,
        mix_weight,
        up_weight,
        down_weight,
        out_weight,
    )
    in_vmem = pl.BlockSpec(memory_space=pltpu.VMEM)
    anywhere = pl.BlockSpec(memory_space=pl.ANY)
    line = n // COLS
    dma = pltpu.SemaphoreType.DMA
    result = pl.pallas_call(
        functools.partial(kernel, n),
        out_shape=jax.ShapeDtypeStruct((rows, patch), F32),
        in_specs=[in_vmem] * 4 + [anywhere] * 9,
        out_specs=in_vmem,
        scratch_shapes=[pltpu.VMEM(w.shape, w.dtype) for w in weights]
        + [
            pltpu.VMEM((ITERS, n * rows, patch), BF16),
            pltpu.VMEM((n * rows, model), BF16),
            pltpu.VMEM((ITERS, TAIL, patch), BF16),
            pltpu.VMEM((ITERS, TAIL, patch), BF16),
            pltpu.VMEM((pairs, 2 * rows, pair), BF16),
            pltpu.VMEM((pairs, 2 * rows, 1), F32),
            pltpu.VMEM((pairs, 2 * rows, 1), F32),
            pltpu.VMEM((pairs, 2 * rows, pair), F32),
            pltpu.VMEM((rows, patch), F32),
            pltpu.VMEM((rows, patch), BF16),
            pltpu.VMEM((rows, patch), BF16),
            dma((len(weights) + 1,)),
            dma((ITERS + 1, 4, line)),
            dma((ITERS + 1, 4, line)),
            dma((ITERS,)),
            dma((ITERS,)),
            dma,
            dma,
        ],
        compiler_params=pltpu.CompilerParams(
            collective_id=0, has_side_effects=True, vmem_limit_bytes=56 * 2**20
        ),
    )(
        latent_noise,
        gain_attn.reshape(1, model),
        gain_mlp.reshape(1, model),
        gain_out.reshape(1, model),
        position,
        *weights,
    )
    return result[::-1]


def solution(mesh):
    in_specs = (P(("groups", "seq"), None), P("seq", None)) + (P(),) * 11
    out_specs = P(("groups", "seq"), None)
    return jax.shard_map(
        per_device, mesh=mesh, in_specs=in_specs, out_specs=out_specs, check_vma=False
    )
```

```python
import functools

import jax
import jax.numpy as jnp
from jax import lax
from jax.experimental import pallas as pl
from jax.experimental.pallas import tpu as pltpu
from jax.sharding import PartitionSpec as P

HEADS = 6
ITERS = 2
COLS = 4
DOWN, ACROSS, CORE, CORE_FAR = range(4)
TAIL = 16
F32, BF16 = jnp.float32, jnp.bfloat16


def dot(a, b):
    return jnp.dot(a, b, preferred_element_type=F32)


def dot_nt(a, b):
    return lax.dot_general(a, b, (((1,), (1,)), ((), ())), preferred_element_type=F32)


def rms_norm(values, gain):
    scale = lax.rsqrt(jnp.mean(values * values, axis=-1, keepdims=True) + 1e-06)
    return values * scale * gain.reshape(1, -1)


def kernel(
    n,
    latent,
    gain_attn,
    gain_mlp,
    gain_out,
    position,
    *refs,
):
    hbm = refs[:8]
    out = refs[8]
    scratch = refs[9:]
    in_w, q_w, k_w, v_w, mix_w, up_w, down_w, out_w = vmem = scratch[:8]
    (
        blocks,
        places,
        tail_src,
        tail_dst,
        queries,
        top,
        total,
        acc,
        noise,
        current,
        flip_src,
        flip_dst,
        load_sem,
        send_sem,
        recv_sem,
        tail_send,
        tail_recv,
        flip_send,
        flip_recv,
    ) = scratch[8:]
    patch, rows = latent.shape
    width = q_w.shape[1]
    head_dim = width // HEADS
    pair = 2 * head_dim
    pairs = HEADS // 2
    line = n // COLS
    me = lax.axis_index("seq")
    row, col = me // COLS, me % COLS
    across = row * COLS + (col + 2) % COLS
    other = me + 1 - 2 * (me % 2)
    mirror = n - 1 - me

    loads = [
        pltpu.make_async_copy(source, target, load_sem.at[i])
        for i, (source, target) in enumerate(zip(hbm, vmem))
    ]
    own_rows = pl.ds(pl.multiple_of(me * rows, rows), rows)
    place_load = pltpu.make_async_copy(position, places.at[own_rows], load_sem.at[len(loads)])
    place_load.start()
    for load in loads:
        load.start()

    barrier = pltpu.get_barrier_semaphore()

    def greet(device):
        pl.semaphore_signal(barrier, inc=1, device_id={"seq": device}, device_id_type=pl.DeviceIdType.MESH)

    greet(across)
    greet(other)
    greet(mirror)
    pl.when(row > 0)(lambda: greet(me - COLS))
    pl.when(row < line - 1)(lambda: greet(me + COLS))
    pl.when(me > 0)(lambda: greet(me - 1))
    pl.when(me < n - 1)(lambda: greet(me + 1))

    def hop(payload, kind, which):
        column = (col + 2) % COLS if kind == CORE_FAR else col
        return remote(payload, kind, which, column)

    def landing(payload, kind, which):
        beside = col + 1 - 2 * (col % 2)
        column = {DOWN: col, ACROSS: (col + 2) % COLS, CORE: beside, CORE_FAR: (beside + 2) % COLS}[kind]
        return remote(payload, kind, which, column)

    def remote(payload, kind, which, column):
        here = pl.ds(pl.multiple_of((which * COLS + column) * rows, rows), rows)
        ref = places.at[here] if payload == ITERS else blocks.at[payload, here]
        target = {DOWN: me + COLS, ACROSS: across, CORE: other, CORE_FAR: other}[kind]
        return pltpu.make_async_remote_copy(
            src_ref=ref,
            dst_ref=ref,
            send_sem=send_sem.at[payload, kind, which],
            recv_sem=recv_sem.at[payload, kind, which],
            device_id={"seq": target},
            device_id_type=pl.DeviceIdType.MESH,
        )

    def send_on(payload, which):
        pl.when(row < line - 1)(lambda: hop(payload, DOWN, which).start())
        hop(payload, ACROSS, which).start()
        hop(payload, CORE, which).start()

    def tail_copy(step):
        return pltpu.make_async_remote_copy(
            src_ref=tail_src.at[step],
            dst_ref=tail_dst.at[step],
            send_sem=tail_send.at[step],
            recv_sem=tail_recv.at[step],
            device_id={"seq": me + 1},
            device_id_type=pl.DeviceIdType.MESH,
        )

    noise[...] = latent[...].T
    current[...] = noise[...]
    place_load.wait()
    pl.semaphore_wait(
        barrier,
        3
        + (row > 0).astype(jnp.int32)
        + (row < line - 1).astype(jnp.int32)
        + (me > 0).astype(jnp.int32)
        + (me < n - 1).astype(jnp.int32),
    )

    lane = lax.broadcasted_iota(jnp.int32, (1, pair), 1)
    low = lane < head_dim

    for step in range(ITERS):
        payloads = (ITERS, 0) if step == 0 else (step,)
        value = current[...]
        tail_src[step] = value[rows - TAIL :].astype(BF16)
        pl.when(me < n - 1)(lambda: tail_copy(step).start())
        if step == 0:
            send_on(ITERS, row)
        turned = pltpu.roll(value, 1, 0)
        pl.when(me > 0)(lambda: tail_copy(step).wait_recv())

        @pl.when(me == 0)
        def _():
            tail_dst[step] = jnp.zeros_like(tail_dst[step])

        before = tail_dst[step].astype(F32)[TAIL - 1 :]
        first = lax.broadcasted_iota(jnp.int32, (rows, 1), 0) == 0
        shifted = jnp.where(first, before, turned).astype(BF16)
        blocks[step, own_rows] = shifted
        send_on(step, row)

        if step == 0:
            for load in loads[:4]:
                load.wait()
        hidden_in = dot(shifted, in_w[...]) + places[own_rows].astype(F32)
        normed = rms_norm(hidden_in, gain_attn[...]).astype(BF16)
        query = dot(normed, q_w[...]).astype(BF16).astype(F32) * head_dim ** (-0.5)
        for p in range(pairs):
            both = query[:, p * pair : (p + 1) * pair]
            queries[p, :rows] = jnp.where(low, both, 0.0).astype(BF16)
            queries[p, rows:] = jnp.where(low, 0.0, both).astype(BF16)

        def take(which):
            for payload in payloads:
                landing(payload, DOWN, which).wait_recv()
                send_on(payload, which)

        def pass_far(which):
            for payload in payloads:
                landing(payload, ACROSS, which).wait_recv()
                hop(payload, CORE_FAR, which).start()

        def gather(which):
            for payload in payloads:
                landing(payload, CORE, which).wait_recv()
                landing(payload, CORE_FAR, which).wait_recv()

        def attend(which, own):
            span = COLS * rows
            here = pl.ds(pl.multiple_of(which * span, span), span)
            hidden = dot(blocks[step, here], in_w[...]) + places[here].astype(F32)
            normed = rms_norm(hidden, gain_attn[...]).astype(BF16)
            keys = dot(normed, k_w[...]).astype(BF16)
            values = dot(normed, v_w[...]).astype(BF16)
            pl.when(which > 0)(lambda: pass_far(which - 1))
            if own:
                query_pos = lax.broadcasted_iota(jnp.int32, (2 * rows, span), 0) % rows + col * rows
                key_pos = lax.broadcasted_iota(jnp.int32, (2 * rows, span), 1)
                causal = key_pos <= query_pos
            for p in range(pairs):
                columns = slice(p * pair, (p + 1) * pair)
                scores = dot_nt(queries[p], keys[:, columns])
                if own:
                    scores = jnp.where(causal, scores, -1e30)
                highest = jnp.max(scores, axis=1, keepdims=True)
                if not own:
                    old = top[p]
                    highest = jnp.maximum(old, highest)
                weights = jnp.exp(scores - highest)
                sums = jnp.sum(weights, axis=1, keepdims=True)
                product = dot(weights.astype(BF16), values[:, columns])
                if own:
                    total[p] = sums
                    acc[p] = product
                else:
                    shrink = jnp.exp(old - highest)
                    total[p] = total[p] * shrink + sums
                    acc[p] = acc[p] * shrink + product
                top[p] = highest

        pass_far(row)
        pl.when(row > 0)(lambda: take(row - 1))
        gather(row)
        attend(row, True)

        @pl.loop(0, row)
        def _(i):
            which = row - 1 - i
            pl.when(which > 0)(lambda: take(which - 1))
            gather(which)
            attend(which, False)

        parts = []
        for p in range(pairs):
            result = acc[p] / total[p]
            parts.append(jnp.where(low, result[:rows], result[rows:]).astype(BF16))
        attended = jnp.concatenate(parts, axis=1)
        if step == 0:
            for load in loads[4:]:
                load.wait()
        hidden_mid = hidden_in + dot(attended, mix_w[...])
        normed_mlp = rms_norm(hidden_mid, gain_mlp[...]).astype(BF16)
        activated = jax.nn.gelu(dot(normed_mlp, up_w[...])).astype(BF16)
        hidden_out = hidden_mid + dot(activated, down_w[...])
        normed_out = rms_norm(hidden_out, gain_out[...]).astype(BF16)
        statistics = dot(normed_out, out_w[...])
        mean_shift = statistics[:, :patch]
        log_scale = pltpu.roll(statistics, patch, 1)[:, :patch]
        current[...] = noise[...] * jnp.exp(log_scale) + mean_shift

    flip_src[...] = current[...].astype(BF16)
    flip = pltpu.make_async_remote_copy(
        src_ref=flip_src,
        dst_ref=flip_dst,
        send_sem=flip_send,
        recv_sem=flip_recv,
        device_id={"seq": mirror},
        device_id_type=pl.DeviceIdType.MESH,
    )
    flip.start()

    for step in range(ITERS):
        pl.when(me < n - 1)(lambda: tail_copy(step).wait_send())

    @pl.loop(0, row + 1)
    def _(which):
        for payload in range(ITERS + 1):
            pl.when(row < line - 1)(lambda: hop(payload, DOWN, which).wait_send())
            for kind in (ACROSS, CORE, CORE_FAR):
                hop(payload, kind, which).wait_send()

    flip.wait()
    from_row = lax.broadcasted_iota(jnp.int32, (rows, rows), 0)
    to_row = lax.broadcasted_iota(jnp.int32, (rows, rows), 1)
    turn = jnp.where(from_row + to_row == rows - 1, 1.0, 0.0).astype(BF16)
    out[...] = lax.dot_general(
        flip_dst[...], turn, (((0,), (0,)), ((), ())), preferred_element_type=F32
    )


def per_device(
    latent_noise,
    position,
    in_weight,
    gain_attn,
    query_weight,
    key_weight,
    value_weight,
    mix_weight,
    gain_mlp,
    up_weight,
    down_weight,
    gain_out,
    out_weight,
):
    n = lax.axis_size("seq")
    rows, patch = latent_noise.shape
    model = position.shape[1]
    pair = 2 * query_weight.shape[1] // HEADS
    pairs = HEADS // 2
    weights = (
        in_weight,
        query_weight,
        key_weight,
        value_weight,
        mix_weight,
        up_weight,
        down_weight,
        out_weight,
    )
    in_vmem = pl.BlockSpec(memory_space=pltpu.VMEM)
    anywhere = pl.BlockSpec(memory_space=pl.ANY)
    line = n // COLS
    dma = pltpu.SemaphoreType.DMA
    result = pl.pallas_call(
        functools.partial(kernel, n),
        out_shape=jax.ShapeDtypeStruct((patch, rows), F32),
        in_specs=[in_vmem] * 4 + [anywhere] * 9,
        out_specs=in_vmem,
        scratch_shapes=[pltpu.VMEM(w.shape, w.dtype) for w in weights]
        + [
            pltpu.VMEM((ITERS, n * rows, patch), BF16),
            pltpu.VMEM((n * rows, model), BF16),
            pltpu.VMEM((ITERS, TAIL, patch), BF16),
            pltpu.VMEM((ITERS, TAIL, patch), BF16),
            pltpu.VMEM((pairs, 2 * rows, pair), BF16),
            pltpu.VMEM((pairs, 2 * rows, 1), F32),
            pltpu.VMEM((pairs, 2 * rows, 1), F32),
            pltpu.VMEM((pairs, 2 * rows, pair), F32),
            pltpu.VMEM((rows, patch), F32),
            pltpu.VMEM((rows, patch), F32),
            pltpu.VMEM((rows, patch), BF16),
            pltpu.VMEM((rows, patch), BF16),
            dma((len(weights) + 1,)),
            dma((ITERS + 1, 4, line)),
            dma((ITERS + 1, 4, line)),
            dma((ITERS,)),
            dma((ITERS,)),
            dma,
            dma,
        ],
        compiler_params=pltpu.CompilerParams(
            collective_id=0, has_side_effects=True, vmem_limit_bytes=56 * 2**20
        ),
    )(
        latent_noise.T,
        gain_attn,
        gain_mlp,
        gain_out,
        position,
        *weights,
    )
    return result.T


def solution(mesh):
    in_specs = (P(("groups", "seq"), None), P("seq", None)) + (P(),) * 11
    out_specs = P(("groups", "seq"), None)
    return jax.shard_map(
        per_device, mesh=mesh, in_specs=in_specs, out_specs=out_specs, check_vma=False
    )
```

```python
import functools

import jax
import jax.numpy as jnp
from jax import lax
from jax.experimental import pallas as pl
from jax.experimental.pallas import tpu as pltpu
from jax.sharding import PartitionSpec as P

HEADS = 6
ITERS = 2
COLS = 4
DOWN, ACROSS, CORE, CORE_FAR = range(4)
TAIL = 16
F32, BF16 = jnp.float32, jnp.bfloat16


def dot(a, b):
    return jnp.dot(a, b, preferred_element_type=F32)


def dot_nt(a, b):
    return lax.dot_general(a, b, (((1,), (1,)), ((), ())), preferred_element_type=F32)


def rms_norm(values, gain):
    scale = lax.rsqrt(jnp.mean(values * values, axis=-1, keepdims=True) + 1e-06)
    return values * scale * gain.reshape(1, -1)


def kernel(
    n,
    latent,
    gain_attn,
    gain_mlp,
    gain_out,
    position,
    *refs,
):
    hbm = refs[:8]
    out = refs[8]
    scratch = refs[9:]
    in_w, q_w, k_w, v_w, mix_w, up_w, down_w, out_w = vmem = scratch[:8]
    (
        blocks,
        places,
        tail_src,
        tail_dst,
        queries,
        top,
        total,
        acc,
        noise,
        current,
        flip_src,
        flip_dst,
        load_sem,
        send_sem,
        recv_sem,
        tail_send,
        tail_recv,
        flip_send,
        flip_recv,
    ) = scratch[8:]
    patch, rows = latent.shape
    width = q_w.shape[1]
    head_dim = width // HEADS
    pair = 2 * head_dim
    pairs = HEADS // 2
    line = n // COLS
    me = lax.axis_index("seq")
    row, col = me // COLS, me % COLS
    across = row * COLS + (col + 2) % COLS
    other = me + 1 - 2 * (me % 2)
    mirror = n - 1 - me

    loads = [
        pltpu.make_async_copy(source, target, load_sem.at[i])
        for i, (source, target) in enumerate(zip(hbm, vmem))
    ]
    own_rows = pl.ds(pl.multiple_of(me * rows, rows), rows)
    place_load = pltpu.make_async_copy(position, places.at[own_rows], load_sem.at[len(loads)])
    place_load.start()
    for load in loads:
        load.start()

    barrier = pltpu.get_barrier_semaphore()

    def greet(device):
        pl.semaphore_signal(barrier, inc=1, device_id={"seq": device}, device_id_type=pl.DeviceIdType.MESH)

    greet(across)
    greet(other)
    greet(mirror)
    pl.when(row > 0)(lambda: greet(me - COLS))
    pl.when(row < line - 1)(lambda: greet(me + COLS))
    pl.when(me > 0)(lambda: greet(me - 1))
    pl.when(me < n - 1)(lambda: greet(me + 1))

    def hop(payload, kind, which):
        column = (col + 2) % COLS if kind == CORE_FAR else col
        return remote(payload, kind, which, column)

    def landing(payload, kind, which):
        beside = col + 1 - 2 * (col % 2)
        column = {DOWN: col, ACROSS: (col + 2) % COLS, CORE: beside, CORE_FAR: (beside + 2) % COLS}[kind]
        return remote(payload, kind, which, column)

    def remote(payload, kind, which, column):
        here = pl.ds(pl.multiple_of((which * COLS + column) * rows, rows), rows)
        ref = places.at[here] if payload == ITERS else blocks.at[payload, here]
        target = {DOWN: me + COLS, ACROSS: across, CORE: other, CORE_FAR: other}[kind]
        return pltpu.make_async_remote_copy(
            src_ref=ref,
            dst_ref=ref,
            send_sem=send_sem.at[payload, kind, which],
            recv_sem=recv_sem.at[payload, kind, which],
            device_id={"seq": target},
            device_id_type=pl.DeviceIdType.MESH,
        )

    def send_on(payload, which):
        pl.when(row < line - 1)(lambda: hop(payload, DOWN, which).start())
        hop(payload, ACROSS, which).start()
        hop(payload, CORE, which).start()

    def tail_copy(step):
        return pltpu.make_async_remote_copy(
            src_ref=tail_src.at[step],
            dst_ref=tail_dst.at[step],
            send_sem=tail_send.at[step],
            recv_sem=tail_recv.at[step],
            device_id={"seq": me + 1},
            device_id_type=pl.DeviceIdType.MESH,
        )

    noise[...] = latent[...].T
    current[...] = noise[...]
    place_load.wait()
    pl.semaphore_wait(
        barrier,
        3
        + (row > 0).astype(jnp.int32)
        + (row < line - 1).astype(jnp.int32)
        + (me > 0).astype(jnp.int32)
        + (me < n - 1).astype(jnp.int32),
    )

    lane = lax.broadcasted_iota(jnp.int32, (1, pair), 1)
    low = lane < head_dim

    for step in range(ITERS):
        payloads = (ITERS, 0) if step == 0 else (step,)
        value = current[...]
        tail_src[step] = value[rows - TAIL :].astype(BF16)
        pl.when(me < n - 1)(lambda: tail_copy(step).start())
        if step == 0:
            send_on(ITERS, row)
        turned = pltpu.roll(value, 1, 0)
        pl.when(me > 0)(lambda: tail_copy(step).wait_recv())

        @pl.when(me == 0)
        def _():
            tail_dst[step] = jnp.zeros_like(tail_dst[step])

        before = tail_dst[step].astype(F32)[TAIL - 1 :]
        first = lax.broadcasted_iota(jnp.int32, (rows, 1), 0) == 0
        shifted = jnp.where(first, before, turned).astype(BF16)
        blocks[step, own_rows] = shifted
        send_on(step, row)

        if step == 0:
            for load in loads[:4]:
                load.wait()
        hidden_in = dot(shifted, in_w[...]) + places[own_rows].astype(F32)
        normed = rms_norm(hidden_in, gain_attn[...]).astype(BF16)
        query = dot(normed, q_w[...]).astype(BF16).astype(F32) * head_dim ** (-0.5)
        for p in range(pairs):
            both = query[:, p * pair : (p + 1) * pair]
            queries[p, :rows] = jnp.where(low, both, 0.0).astype(BF16)
            queries[p, rows:] = jnp.where(low, 0.0, both).astype(BF16)

        def take(which):
            for payload in payloads:
                landing(payload, DOWN, which).wait_recv()
                send_on(payload, which)

        def pass_far(which):
            for payload in payloads:
                landing(payload, ACROSS, which).wait_recv()
                hop(payload, CORE_FAR, which).start()

        def gather(which):
            for payload in payloads:
                landing(payload, CORE, which).wait_recv()
                landing(payload, CORE_FAR, which).wait_recv()

        def attend(which, own):
            span = COLS * rows
            here = pl.ds(pl.multiple_of(which * span, span), span)
            hidden = dot(blocks[step, here], in_w[...]) + places[here].astype(F32)
            normed = rms_norm(hidden, gain_attn[...]).astype(BF16)
            keys = dot(normed, k_w[...]).astype(BF16)
            values = dot(normed, v_w[...]).astype(BF16)
            if step > 0:
                pl.when(which > 0)(lambda: pass_far(which - 1))
            if own:
                query_pos = lax.broadcasted_iota(jnp.int32, (2 * rows, span), 0) % rows + col * rows
                key_pos = lax.broadcasted_iota(jnp.int32, (2 * rows, span), 1)
                causal = key_pos <= query_pos
            for p in range(pairs):
                columns = slice(p * pair, (p + 1) * pair)
                scores = dot_nt(queries[p], keys[:, columns])
                if own:
                    scores = jnp.where(causal, scores, -1e30)
                highest = jnp.max(scores, axis=1, keepdims=True)
                if not own:
                    old = top[p]
                    highest = jnp.maximum(old, highest)
                weights = jnp.exp(scores - highest)
                sums = jnp.sum(weights, axis=1, keepdims=True)
                product = dot(weights.astype(BF16), values[:, columns])
                if own:
                    total[p] = sums
                    acc[p] = product
                else:
                    shrink = jnp.exp(old - highest)
                    total[p] = total[p] * shrink + sums
                    acc[p] = acc[p] * shrink + product
                top[p] = highest

        pass_far(row)
        pl.when(row > 0)(lambda: take(row - 1))
        gather(row)
        attend(row, True)

        @pl.loop(0, row)
        def _(i):
            which = row - 1 - i
            if step == 0:
                pass_far(which)
            pl.when(which > 0)(lambda: take(which - 1))
            gather(which)
            attend(which, False)

        parts = []
        for p in range(pairs):
            result = acc[p] / total[p]
            parts.append(jnp.where(low, result[:rows], result[rows:]).astype(BF16))
        attended = jnp.concatenate(parts, axis=1)
        if step == 0:
            for load in loads[4:]:
                load.wait()
        hidden_mid = hidden_in + dot(attended, mix_w[...])
        normed_mlp = rms_norm(hidden_mid, gain_mlp[...]).astype(BF16)
        activated = jax.nn.gelu(dot(normed_mlp, up_w[...])).astype(BF16)
        hidden_out = hidden_mid + dot(activated, down_w[...])
        normed_out = rms_norm(hidden_out, gain_out[...]).astype(BF16)
        statistics = dot(normed_out, out_w[...])
        mean_shift = statistics[:, :patch]
        log_scale = pltpu.roll(statistics, patch, 1)[:, :patch]
        current[...] = noise[...] * jnp.exp(log_scale) + mean_shift

    flip_src[...] = current[...].astype(BF16)
    flip = pltpu.make_async_remote_copy(
        src_ref=flip_src,
        dst_ref=flip_dst,
        send_sem=flip_send,
        recv_sem=flip_recv,
        device_id={"seq": mirror},
        device_id_type=pl.DeviceIdType.MESH,
    )
    flip.start()

    for step in range(ITERS):
        pl.when(me < n - 1)(lambda: tail_copy(step).wait_send())

    @pl.loop(0, row + 1)
    def _(which):
        for payload in range(ITERS + 1):
            pl.when(row < line - 1)(lambda: hop(payload, DOWN, which).wait_send())
            for kind in (ACROSS, CORE, CORE_FAR):
                hop(payload, kind, which).wait_send()

    flip.wait()
    from_row = lax.broadcasted_iota(jnp.int32, (rows, rows), 0)
    to_row = lax.broadcasted_iota(jnp.int32, (rows, rows), 1)
    turn = jnp.where(from_row + to_row == rows - 1, 1.0, 0.0).astype(BF16)
    out[...] = lax.dot_general(
        flip_dst[...], turn, (((0,), (0,)), ((), ())), preferred_element_type=F32
    )


def per_device(
    latent_noise,
    position,
    in_weight,
    gain_attn,
    query_weight,
    key_weight,
    value_weight,
    mix_weight,
    gain_mlp,
    up_weight,
    down_weight,
    gain_out,
    out_weight,
):
    n = lax.axis_size("seq")
    rows, patch = latent_noise.shape
    model = position.shape[1]
    pair = 2 * query_weight.shape[1] // HEADS
    pairs = HEADS // 2
    weights = (
        in_weight,
        query_weight,
        key_weight,
        value_weight,
        mix_weight,
        up_weight,
        down_weight,
        out_weight,
    )
    in_vmem = pl.BlockSpec(memory_space=pltpu.VMEM)
    anywhere = pl.BlockSpec(memory_space=pl.ANY)
    line = n // COLS
    dma = pltpu.SemaphoreType.DMA
    result = pl.pallas_call(
        functools.partial(kernel, n),
        out_shape=jax.ShapeDtypeStruct((patch, rows), F32),
        in_specs=[in_vmem] * 4 + [anywhere] * 9,
        out_specs=in_vmem,
        scratch_shapes=[pltpu.VMEM(w.shape, w.dtype) for w in weights]
        + [
            pltpu.VMEM((ITERS, n * rows, patch), BF16),
            pltpu.VMEM((n * rows, model), BF16),
            pltpu.VMEM((ITERS, TAIL, patch), BF16),
            pltpu.VMEM((ITERS, TAIL, patch), BF16),
            pltpu.VMEM((pairs, 2 * rows, pair), BF16),
            pltpu.VMEM((pairs, 2 * rows, 1), F32),
            pltpu.VMEM((pairs, 2 * rows, 1), F32),
            pltpu.VMEM((pairs, 2 * rows, pair), F32),
            pltpu.VMEM((rows, patch), F32),
            pltpu.VMEM((rows, patch), F32),
            pltpu.VMEM((rows, patch), BF16),
            pltpu.VMEM((rows, patch), BF16),
            dma((len(weights) + 1,)),
            dma((ITERS + 1, 4, line)),
            dma((ITERS + 1, 4, line)),
            dma((ITERS,)),
            dma((ITERS,)),
            dma,
            dma,
        ],
        compiler_params=pltpu.CompilerParams(
            collective_id=0, has_side_effects=True, vmem_limit_bytes=56 * 2**20
        ),
    )(
        latent_noise.T,
        gain_attn,
        gain_mlp,
        gain_out,
        position,
        *weights,
    )
    return result.T


def solution(mesh):
    in_specs = (P(("groups", "seq"), None), P("seq", None)) + (P(),) * 11
    out_specs = P(("groups", "seq"), None)
    return jax.shard_map(
        per_device, mesh=mesh, in_specs=in_specs, out_specs=out_specs, check_vma=False
    )
```

```python
import functools

import jax
import jax.numpy as jnp
from jax import lax
from jax.experimental import pallas as pl
from jax.experimental.pallas import tpu as pltpu
from jax.sharding import PartitionSpec as P

HEADS = 6
ITERS = 2
COLS = 4
DOWN, ACROSS, CORE, CORE_FAR, SIDE = range(5)
TAIL = 16
F32, BF16 = jnp.float32, jnp.bfloat16


def dot(a, b):
    return jnp.dot(a, b, preferred_element_type=F32)


def dot_nt(a, b):
    return lax.dot_general(a, b, (((1,), (1,)), ((), ())), preferred_element_type=F32)


def rms_norm(values, gain):
    scale = lax.rsqrt(jnp.mean(values * values, axis=-1, keepdims=True) + 1e-06)
    return values * scale * gain.reshape(1, -1)


def kernel(
    n,
    split,
    latent,
    gain_attn,
    gain_mlp,
    gain_out,
    position,
    *refs,
):
    hbm = refs[:8]
    out = refs[8]
    scratch = refs[9:]
    in_w, q_w, k_w, v_w, mix_w, up_w, down_w, out_w = vmem = scratch[:8]
    (
        blocks,
        places,
        tail_src,
        tail_dst,
        queries,
        top,
        total,
        acc,
        noise,
        current,
        flip_src,
        flip_dst,
        load_sem,
        send_sem,
        recv_sem,
        tail_send,
        tail_recv,
        flip_send,
        flip_recv,
    ) = scratch[8:]
    patch, rows = latent.shape
    width = q_w.shape[1]
    head_dim = width // HEADS
    pair = 2 * head_dim
    pairs = HEADS // 2
    line = n // COLS
    me = lax.axis_index("seq")
    row, col = me // COLS, me % COLS
    across = row * COLS + (col + 2) % COLS
    other = me + 1 - 2 * (me % 2)
    mirror = n - 1 - me
    group = lax.axis_index("groups")
    half = group % 2
    partner = group + 1 - 2 * half

    loads = [
        pltpu.make_async_copy(source, target, load_sem.at[i])
        for i, (source, target) in enumerate(zip(hbm, vmem))
    ]
    own_rows = pl.ds(pl.multiple_of(me * rows, rows), rows)
    place_load = pltpu.make_async_copy(position, places.at[own_rows], load_sem.at[len(loads)])
    place_load.start()
    for load in loads:
        load.start()

    barrier = pltpu.get_barrier_semaphore()

    def greet(device):
        pl.semaphore_signal(barrier, inc=1, device_id={"seq": device}, device_id_type=pl.DeviceIdType.MESH)

    greet(across)
    greet(other)
    greet(mirror)
    if split:
        pl.semaphore_signal(
            barrier, inc=1, device_id={"groups": partner}, device_id_type=pl.DeviceIdType.MESH
        )
    pl.when(row > 0)(lambda: greet(me - COLS))
    pl.when(row < line - 1)(lambda: greet(me + COLS))
    pl.when(me > 0)(lambda: greet(me - 1))
    pl.when(me < n - 1)(lambda: greet(me + 1))

    def hop(payload, kind, which):
        column = (col + 2) % COLS if kind in (CORE_FAR, SIDE) else col
        return remote(payload, kind, which, column, half)

    def landing(payload, kind, which):
        beside = col + 1 - 2 * (col % 2)
        column = {DOWN: col, ACROSS: (col + 2) % COLS, SIDE: (col + 2) % COLS, CORE: beside, CORE_FAR: (beside + 2) % COLS}[kind]
        return remote(payload, kind, which, column, 1 - half if kind == SIDE else half)

    def remote(payload, kind, which, column, share):
        here = pl.ds(pl.multiple_of((which * COLS + column) * rows, rows), rows)
        ref = places.at[here] if payload == ITERS else blocks.at[payload, here]
        if payload == ITERS and split and kind in (ACROSS, SIDE):
            part = places.shape[1] // 2
            ref = places.at[here, pl.ds(pl.multiple_of(share * part, part), part)]
        target = {DOWN: me + COLS, ACROSS: across, CORE: other, CORE_FAR: other, SIDE: None}[kind]
        device = {"groups": partner} if kind == SIDE else {"seq": target}
        return pltpu.make_async_remote_copy(
            src_ref=ref,
            dst_ref=ref,
            send_sem=send_sem.at[payload, kind, which],
            recv_sem=recv_sem.at[payload, kind, which],
            device_id=device,
            device_id_type=pl.DeviceIdType.MESH,
        )

    def send_on(payload, which):
        pl.when(row < line - 1)(lambda: hop(payload, DOWN, which).start())
        hop(payload, ACROSS, which).start()
        hop(payload, CORE, which).start()

    def tail_copy(step):
        return pltpu.make_async_remote_copy(
            src_ref=tail_src.at[step],
            dst_ref=tail_dst.at[step],
            send_sem=tail_send.at[step],
            recv_sem=tail_recv.at[step],
            device_id={"seq": me + 1},
            device_id_type=pl.DeviceIdType.MESH,
        )

    noise[...] = latent[...].T
    current[...] = noise[...]
    place_load.wait()
    pl.semaphore_wait(
        barrier,
        (4 if split else 3)
        + (row > 0).astype(jnp.int32)
        + (row < line - 1).astype(jnp.int32)
        + (me > 0).astype(jnp.int32)
        + (me < n - 1).astype(jnp.int32),
    )

    lane = lax.broadcasted_iota(jnp.int32, (1, pair), 1)
    low = lane < head_dim

    for step in range(ITERS):
        payloads = (ITERS, 0) if step == 0 else (step,)
        value = current[...]
        tail_src[step] = value[rows - TAIL :].astype(BF16)
        pl.when(me < n - 1)(lambda: tail_copy(step).start())
        if step == 0:
            send_on(ITERS, row)
        turned = pltpu.roll(value, 1, 0)
        pl.when(me > 0)(lambda: tail_copy(step).wait_recv())

        @pl.when(me == 0)
        def _():
            tail_dst[step] = jnp.zeros_like(tail_dst[step])

        before = tail_dst[step].astype(F32)[TAIL - 1 :]
        first = lax.broadcasted_iota(jnp.int32, (rows, 1), 0) == 0
        shifted = jnp.where(first, before, turned).astype(BF16)
        blocks[step, own_rows] = shifted
        send_on(step, row)

        if step == 0:
            for load in loads[:4]:
                load.wait()
        hidden_in = dot(shifted, in_w[...]) + places[own_rows].astype(F32)
        normed = rms_norm(hidden_in, gain_attn[...]).astype(BF16)
        query = dot(normed, q_w[...]).astype(BF16).astype(F32) * head_dim ** (-0.5)
        for p in range(pairs):
            both = query[:, p * pair : (p + 1) * pair]
            queries[p, :rows] = jnp.where(low, both, 0.0).astype(BF16)
            queries[p, rows:] = jnp.where(low, 0.0, both).astype(BF16)

        def take(which):
            for payload in payloads:
                landing(payload, DOWN, which).wait_recv()
                send_on(payload, which)

        def pass_far(which):
            for payload in payloads:
                landing(payload, ACROSS, which).wait_recv()
                hop(payload, CORE_FAR, which).start()

        def sideways(which):
            landing(ITERS, ACROSS, which).wait_recv()
            hop(ITERS, SIDE, which).start()
            landing(0, ACROSS, which).wait_recv()
            hop(0, CORE_FAR, which).start()
            pl.when(which > 0)(lambda: take(which - 1))
            landing(ITERS, SIDE, which).wait_recv()
            hop(ITERS, CORE_FAR, which).start()

        def gather(which):
            for payload in payloads:
                landing(payload, CORE, which).wait_recv()
                landing(payload, CORE_FAR, which).wait_recv()

        def attend(which, own):
            span = COLS * rows
            here = pl.ds(pl.multiple_of(which * span, span), span)
            hidden = dot(blocks[step, here], in_w[...]) + places[here].astype(F32)
            normed = rms_norm(hidden, gain_attn[...]).astype(BF16)
            keys = dot(normed, k_w[...]).astype(BF16)
            values = dot(normed, v_w[...]).astype(BF16)
            if step > 0:
                pl.when(which > 0)(lambda: pass_far(which - 1))
            if own:
                query_pos = lax.broadcasted_iota(jnp.int32, (2 * rows, span), 0) % rows + col * rows
                key_pos = lax.broadcasted_iota(jnp.int32, (2 * rows, span), 1)
                causal = key_pos <= query_pos
            for p in range(pairs):
                columns = slice(p * pair, (p + 1) * pair)
                scores = dot_nt(queries[p], keys[:, columns])
                if own:
                    scores = jnp.where(causal, scores, -1e30)
                highest = jnp.max(scores, axis=1, keepdims=True)
                if not own:
                    old = top[p]
                    highest = jnp.maximum(old, highest)
                weights = jnp.exp(scores - highest)
                sums = jnp.sum(weights, axis=1, keepdims=True)
                product = dot(weights.astype(BF16), values[:, columns])
                if own:
                    total[p] = sums
                    acc[p] = product
                else:
                    shrink = jnp.exp(old - highest)
                    total[p] = total[p] * shrink + sums
                    acc[p] = acc[p] * shrink + product
                top[p] = highest

        if step == 0 and split:
            sideways(row)
        else:
            pass_far(row)
            pl.when(row > 0)(lambda: take(row - 1))
        gather(row)
        attend(row, True)

        @pl.loop(0, row)
        def _(i):
            which = row - 1 - i
            if step == 0 and split:
                sideways(which)
            else:
                if step == 0:
                    pass_far(which)
                pl.when(which > 0)(lambda: take(which - 1))
            gather(which)
            attend(which, False)

        parts = []
        for p in range(pairs):
            result = acc[p] / total[p]
            parts.append(jnp.where(low, result[:rows], result[rows:]).astype(BF16))
        attended = jnp.concatenate(parts, axis=1)
        if step == 0:
            for load in loads[4:]:
                load.wait()
        hidden_mid = hidden_in + dot(attended, mix_w[...])
        normed_mlp = rms_norm(hidden_mid, gain_mlp[...]).astype(BF16)
        activated = jax.nn.gelu(dot(normed_mlp, up_w[...])).astype(BF16)
        hidden_out = hidden_mid + dot(activated, down_w[...])
        normed_out = rms_norm(hidden_out, gain_out[...]).astype(BF16)
        statistics = dot(normed_out, out_w[...])
        mean_shift = statistics[:, :patch]
        log_scale = pltpu.roll(statistics, patch, 1)[:, :patch]
        current[...] = noise[...] * jnp.exp(log_scale) + mean_shift

    flip_src[...] = current[...].astype(BF16)
    flip = pltpu.make_async_remote_copy(
        src_ref=flip_src,
        dst_ref=flip_dst,
        send_sem=flip_send,
        recv_sem=flip_recv,
        device_id={"seq": mirror},
        device_id_type=pl.DeviceIdType.MESH,
    )
    flip.start()

    for step in range(ITERS):
        pl.when(me < n - 1)(lambda: tail_copy(step).wait_send())

    @pl.loop(0, row + 1)
    def _(which):
        for payload in range(ITERS + 1):
            pl.when(row < line - 1)(lambda: hop(payload, DOWN, which).wait_send())
            for kind in (ACROSS, CORE, CORE_FAR):
                hop(payload, kind, which).wait_send()
        if split:
            hop(ITERS, SIDE, which).wait_send()

    flip.wait()
    from_row = lax.broadcasted_iota(jnp.int32, (rows, rows), 0)
    to_row = lax.broadcasted_iota(jnp.int32, (rows, rows), 1)
    turn = jnp.where(from_row + to_row == rows - 1, 1.0, 0.0).astype(BF16)
    out[...] = lax.dot_general(
        flip_dst[...], turn, (((0,), (0,)), ((), ())), preferred_element_type=F32
    )


def per_device(
    latent_noise,
    position,
    in_weight,
    gain_attn,
    query_weight,
    key_weight,
    value_weight,
    mix_weight,
    gain_mlp,
    up_weight,
    down_weight,
    gain_out,
    out_weight,
):
    n = lax.axis_size("seq")
    rows, patch = latent_noise.shape
    model = position.shape[1]
    pair = 2 * query_weight.shape[1] // HEADS
    pairs = HEADS // 2
    weights = (
        in_weight,
        query_weight,
        key_weight,
        value_weight,
        mix_weight,
        up_weight,
        down_weight,
        out_weight,
    )
    in_vmem = pl.BlockSpec(memory_space=pltpu.VMEM)
    anywhere = pl.BlockSpec(memory_space=pl.ANY)
    line = n // COLS
    dma = pltpu.SemaphoreType.DMA
    result = pl.pallas_call(
        functools.partial(kernel, n, lax.axis_size("groups") % 2 == 0),
        out_shape=jax.ShapeDtypeStruct((patch, rows), F32),
        in_specs=[in_vmem] * 4 + [anywhere] * 9,
        out_specs=in_vmem,
        scratch_shapes=[pltpu.VMEM(w.shape, w.dtype) for w in weights]
        + [
            pltpu.VMEM((ITERS, n * rows, patch), BF16),
            pltpu.VMEM((n * rows, model), BF16),
            pltpu.VMEM((ITERS, TAIL, patch), BF16),
            pltpu.VMEM((ITERS, TAIL, patch), BF16),
            pltpu.VMEM((pairs, 2 * rows, pair), BF16),
            pltpu.VMEM((pairs, 2 * rows, 1), F32),
            pltpu.VMEM((pairs, 2 * rows, 1), F32),
            pltpu.VMEM((pairs, 2 * rows, pair), F32),
            pltpu.VMEM((rows, patch), F32),
            pltpu.VMEM((rows, patch), F32),
            pltpu.VMEM((rows, patch), BF16),
            pltpu.VMEM((rows, patch), BF16),
            dma((len(weights) + 1,)),
            dma((ITERS + 1, 5, line)),
            dma((ITERS + 1, 5, line)),
            dma((ITERS,)),
            dma((ITERS,)),
            dma,
            dma,
        ],
        compiler_params=pltpu.CompilerParams(
            collective_id=0, has_side_effects=True, vmem_limit_bytes=56 * 2**20
        ),
    )(
        latent_noise.T,
        gain_attn,
        gain_mlp,
        gain_out,
        position,
        *weights,
    )
    return result.T


def solution(mesh):
    in_specs = (P(("groups", "seq"), None), P("seq", None)) + (P(),) * 11
    out_specs = P(("groups", "seq"), None)
    return jax.shard_map(
        per_device, mesh=mesh, in_specs=in_specs, out_specs=out_specs, check_vma=False
    )
```

```python
import functools

import jax
import jax.numpy as jnp
from jax import lax
from jax.experimental import pallas as pl
from jax.experimental.pallas import tpu as pltpu
from jax.sharding import PartitionSpec as P

HEADS = 6
ITERS = 2
COLS = 4
DOWN, ACROSS, CORE, CORE_FAR = range(4)
TAIL = 16
F32, BF16 = jnp.float32, jnp.bfloat16


def dot(a, b):
    return jnp.dot(a, b, preferred_element_type=F32)


def dot_nt(a, b):
    return lax.dot_general(a, b, (((1,), (1,)), ((), ())), preferred_element_type=F32)


def rms_norm(values, gain):
    scale = lax.rsqrt(jnp.mean(values * values, axis=-1, keepdims=True) + 1e-06)
    return values * scale * gain.reshape(1, -1)


def kernel(
    n,
    latent,
    gain_attn,
    gain_mlp,
    gain_out,
    position,
    *refs,
):
    hbm = refs[:8]
    out = refs[8]
    scratch = refs[9:]
    in_w, q_w, k_w, v_w, mix_w, up_w, down_w, out_w = vmem = scratch[:8]
    (
        blocks,
        places,
        tail_src,
        tail_dst,
        queries,
        top,
        total,
        acc,
        noise,
        current,
        flip_src,
        flip_dst,
        load_sem,
        send_sem,
        recv_sem,
        tail_send,
        tail_recv,
        flip_send,
        flip_recv,
    ) = scratch[8:]
    patch, rows = latent.shape
    width = q_w.shape[1]
    head_dim = width // HEADS
    pair = 2 * head_dim
    pairs = HEADS // 2
    line = n // COLS
    me = lax.axis_index("seq")
    row, col = me // COLS, me % COLS
    across = row * COLS + (col + 2) % COLS
    other = me + 1 - 2 * (me % 2)
    mirror = n - 1 - me

    loads = [
        pltpu.make_async_copy(source, target, load_sem.at[i])
        for i, (source, target) in enumerate(zip(hbm, vmem))
    ]
    own_rows = pl.ds(pl.multiple_of(me * rows, rows), rows)
    place_load = pltpu.make_async_copy(position, places.at[own_rows], load_sem.at[len(loads)])
    place_load.start()
    for load in loads:
        load.start()

    barrier = pltpu.get_barrier_semaphore()

    def greet(device):
        pl.semaphore_signal(barrier, inc=1, device_id={"seq": device}, device_id_type=pl.DeviceIdType.MESH)

    greet(across)
    greet(other)
    greet(mirror)
    pl.when(row > 0)(lambda: greet(me - COLS))
    pl.when(row < line - 1)(lambda: greet(me + COLS))
    pl.when(me > 0)(lambda: greet(me - 1))
    pl.when(me < n - 1)(lambda: greet(me + 1))

    def hop(payload, kind, which):
        column = (col + 2) % COLS if kind == CORE_FAR else col
        return remote(payload, kind, which, column)

    def landing(payload, kind, which):
        beside = col + 1 - 2 * (col % 2)
        column = {DOWN: col, ACROSS: (col + 2) % COLS, CORE: beside, CORE_FAR: (beside + 2) % COLS}[kind]
        return remote(payload, kind, which, column)

    def remote(payload, kind, which, column):
        here = pl.ds(pl.multiple_of((which * COLS + column) * rows, rows), rows)
        ref = places.at[here] if payload == ITERS else blocks.at[payload, here]
        target = {DOWN: me + COLS, ACROSS: across, CORE: other, CORE_FAR: other}[kind]
        return pltpu.make_async_remote_copy(
            src_ref=ref,
            dst_ref=ref,
            send_sem=send_sem.at[payload, kind, which],
            recv_sem=recv_sem.at[payload, kind, which],
            device_id={"seq": target},
            device_id_type=pl.DeviceIdType.MESH,
        )

    def send_on(payload, which):
        pl.when(row < line - 1)(lambda: hop(payload, DOWN, which).start())
        hop(payload, ACROSS, which).start()
        hop(payload, CORE, which).start()

    def tail_copy(step):
        return pltpu.make_async_remote_copy(
            src_ref=tail_src.at[step],
            dst_ref=tail_dst.at[step],
            send_sem=tail_send.at[step],
            recv_sem=tail_recv.at[step],
            device_id={"seq": me + 1},
            device_id_type=pl.DeviceIdType.MESH,
        )

    noise[...] = latent[...].T
    current[...] = noise[...]
    place_load.wait()
    pl.semaphore_wait(
        barrier,
        3
        + (row > 0).astype(jnp.int32)
        + (row < line - 1).astype(jnp.int32)
        + (me > 0).astype(jnp.int32)
        + (me < n - 1).astype(jnp.int32),
    )

    lane = lax.broadcasted_iota(jnp.int32, (1, pair), 1)
    low = lane < head_dim

    for step in range(ITERS):
        payloads = (ITERS, 0) if step == 0 else (step,)
        value = current[...]
        tail_src[step] = value[rows - TAIL :].astype(BF16)
        pl.when(me < n - 1)(lambda: tail_copy(step).start())
        if step == 0:
            send_on(ITERS, row)
        turned = pltpu.roll(value, 1, 0)
        pl.when(me > 0)(lambda: tail_copy(step).wait_recv())

        @pl.when(me == 0)
        def _():
            tail_dst[step] = jnp.zeros_like(tail_dst[step])

        before = tail_dst[step].astype(F32)[TAIL - 1 :]
        first = lax.broadcasted_iota(jnp.int32, (rows, 1), 0) == 0
        shifted = jnp.where(first, before, turned).astype(BF16)
        blocks[step, own_rows] = shifted
        send_on(step, row)

        if step == 0:
            for load in loads[:4]:
                load.wait()
        hidden_in = dot(shifted, in_w[...]) + places[own_rows].astype(F32)
        normed = rms_norm(hidden_in, gain_attn[...]).astype(BF16)
        query = dot(normed, q_w[...]).astype(BF16).astype(F32) * head_dim ** (-0.5)
        for p in range(pairs):
            both = query[:, p * pair : (p + 1) * pair]
            queries[p, :rows] = jnp.where(low, both, 0.0).astype(BF16)
            queries[p, rows:] = jnp.where(low, 0.0, both).astype(BF16)

        def take(which):
            for payload in payloads:
                landing(payload, DOWN, which).wait_recv()
                send_on(payload, which)

        def pass_far(which):
            for payload in payloads:
                landing(payload, ACROSS, which).wait_recv()
                hop(payload, CORE_FAR, which).start()

        def gather(which):
            for payload in payloads:
                landing(payload, CORE, which).wait_recv()
                landing(payload, CORE_FAR, which).wait_recv()

        def attend(which, own):
            span = COLS * rows
            here = pl.ds(pl.multiple_of(which * span, span), span)
            hidden = dot(blocks[step, here], in_w[...]) + places[here].astype(F32)
            normed = rms_norm(hidden, gain_attn[...]).astype(BF16)
            keys = dot(normed, k_w[...]).astype(BF16)
            values = dot(normed, v_w[...]).astype(BF16)
            if step > 0:
                pl.when(which > 0)(lambda: pass_far(which - 1))
            if own:
                query_pos = lax.broadcasted_iota(jnp.int32, (2 * rows, span), 0) % rows + col * rows
                key_pos = lax.broadcasted_iota(jnp.int32, (2 * rows, span), 1)
                causal = key_pos <= query_pos
            for p in range(pairs):
                columns = slice(p * pair, (p + 1) * pair)
                scores = dot_nt(queries[p], keys[:, columns])
                if own:
                    scores = jnp.where(causal, scores, -1e30)
                highest = jnp.max(scores, axis=1, keepdims=True)
                if not own:
                    old = top[p]
                    highest = jnp.maximum(old, highest)
                weights = jnp.exp(scores - highest)
                sums = jnp.sum(weights, axis=1, keepdims=True)
                product = dot(weights.astype(BF16), values[:, columns])
                if own:
                    total[p] = sums
                    acc[p] = product
                else:
                    shrink = jnp.exp(old - highest)
                    total[p] = total[p] * shrink + sums
                    acc[p] = acc[p] * shrink + product
                top[p] = highest

        if step > 0:
            pass_far(row)
        pl.when(row > 0)(lambda: take(row - 1))
        if step == 0:
            pass_far(row)
        gather(row)
        attend(row, True)

        @pl.loop(0, row)
        def _(i):
            which = row - 1 - i
            pl.when(which > 0)(lambda: take(which - 1))
            if step == 0:
                pass_far(which)
            gather(which)
            attend(which, False)

        parts = []
        for p in range(pairs):
            result = acc[p] / total[p]
            parts.append(jnp.where(low, result[:rows], result[rows:]).astype(BF16))
        attended = jnp.concatenate(parts, axis=1)
        if step == 0:
            for load in loads[4:]:
                load.wait()
        hidden_mid = hidden_in + dot(attended, mix_w[...])
        normed_mlp = rms_norm(hidden_mid, gain_mlp[...]).astype(BF16)
        activated = jax.nn.gelu(dot(normed_mlp, up_w[...])).astype(BF16)
        hidden_out = hidden_mid + dot(activated, down_w[...])
        normed_out = rms_norm(hidden_out, gain_out[...]).astype(BF16)
        statistics = dot(normed_out, out_w[...])
        mean_shift = statistics[:, :patch]
        log_scale = pltpu.roll(statistics, patch, 1)[:, :patch]
        current[...] = noise[...] * jnp.exp(log_scale) + mean_shift

    flip_src[...] = current[...].astype(BF16)
    flip = pltpu.make_async_remote_copy(
        src_ref=flip_src,
        dst_ref=flip_dst,
        send_sem=flip_send,
        recv_sem=flip_recv,
        device_id={"seq": mirror},
        device_id_type=pl.DeviceIdType.MESH,
    )
    flip.start()

    for step in range(ITERS):
        pl.when(me < n - 1)(lambda: tail_copy(step).wait_send())

    @pl.loop(0, row + 1)
    def _(which):
        for payload in range(ITERS + 1):
            pl.when(row < line - 1)(lambda: hop(payload, DOWN, which).wait_send())
            for kind in (ACROSS, CORE, CORE_FAR):
                hop(payload, kind, which).wait_send()

    flip.wait()
    from_row = lax.broadcasted_iota(jnp.int32, (rows, rows), 0)
    to_row = lax.broadcasted_iota(jnp.int32, (rows, rows), 1)
    turn = jnp.where(from_row + to_row == rows - 1, 1.0, 0.0).astype(BF16)
    out[...] = lax.dot_general(
        flip_dst[...], turn, (((0,), (0,)), ((), ())), preferred_element_type=F32
    )


def per_device(
    latent_noise,
    position,
    in_weight,
    gain_attn,
    query_weight,
    key_weight,
    value_weight,
    mix_weight,
    gain_mlp,
    up_weight,
    down_weight,
    gain_out,
    out_weight,
):
    n = lax.axis_size("seq")
    rows, patch = latent_noise.shape
    model = position.shape[1]
    pair = 2 * query_weight.shape[1] // HEADS
    pairs = HEADS // 2
    weights = (
        in_weight,
        query_weight,
        key_weight,
        value_weight,
        mix_weight,
        up_weight,
        down_weight,
        out_weight,
    )
    in_vmem = pl.BlockSpec(memory_space=pltpu.VMEM)
    anywhere = pl.BlockSpec(memory_space=pl.ANY)
    line = n // COLS
    dma = pltpu.SemaphoreType.DMA
    result = pl.pallas_call(
        functools.partial(kernel, n),
        out_shape=jax.ShapeDtypeStruct((patch, rows), F32),
        in_specs=[in_vmem] * 4 + [anywhere] * 9,
        out_specs=in_vmem,
        scratch_shapes=[pltpu.VMEM(w.shape, w.dtype) for w in weights]
        + [
            pltpu.VMEM((ITERS, n * rows, patch), BF16),
            pltpu.VMEM((n * rows, model), BF16),
            pltpu.VMEM((ITERS, TAIL, patch), BF16),
            pltpu.VMEM((ITERS, TAIL, patch), BF16),
            pltpu.VMEM((pairs, 2 * rows, pair), BF16),
            pltpu.VMEM((pairs, 2 * rows, 1), F32),
            pltpu.VMEM((pairs, 2 * rows, 1), F32),
            pltpu.VMEM((pairs, 2 * rows, pair), F32),
            pltpu.VMEM((rows, patch), F32),
            pltpu.VMEM((rows, patch), F32),
            pltpu.VMEM((rows, patch), BF16),
            pltpu.VMEM((rows, patch), BF16),
            dma((len(weights) + 1,)),
            dma((ITERS + 1, 4, line)),
            dma((ITERS + 1, 4, line)),
            dma((ITERS,)),
            dma((ITERS,)),
            dma,
            dma,
        ],
        compiler_params=pltpu.CompilerParams(
            collective_id=0, has_side_effects=True, vmem_limit_bytes=56 * 2**20
        ),
    )(
        latent_noise.T,
        gain_attn,
        gain_mlp,
        gain_out,
        position,
        *weights,
    )
    return result.T


def solution(mesh):
    in_specs = (P(("groups", "seq"), None), P("seq", None)) + (P(),) * 11
    out_specs = P(("groups", "seq"), None)
    return jax.shard_map(
        per_device, mesh=mesh, in_specs=in_specs, out_specs=out_specs, check_vma=False
    )
```
